32 devices in a mesh: grp: 2 (over x), ex: 16 (over z, y, core).
Axes of the slice: x: 2, y: 2, z: 4, core: 2. Of those that a mesh axis runs over, the one named last changes fastest.
Arguments:
- layer_input: bfloat16 [4096, 2048], P(('grp', 'ex')), parts along dimension 0, may hold values from -6 to 6
- cotangent: bfloat16 [4096, 256], P(('grp', 'ex')), parts along dimension 0, may hold values from -6 to 6
- example_weight: bfloat16 [32], P('ex'), may hold values from 0.3984375 to 4
Outputs:
- kernel: float32 [64, 32], P(('grp', 'ex')), parts along dimension 0
- sq_norms: float32 [64], P(('grp', 'ex')), parts along dimension 0
The draws below stay inside these ranges and needn't reach their ends.
There are 2 independent parts, one for each index of `grp`. The reference program is written for one: setup_inputs(seed, part) draws one part's arguments, and reference() takes and returns one part's arrays. A program takes and returns all parts, laid end to end along the dimension named above; an argument that names none is the same for every part. Nothing has to cross between parts.
All inputs are finite; a program needn't handle non-finite values.
Results may differ from the reference program's by a relative error of at most 0.0003.
Values may be sent and summed in bfloat16 or wider, within the bound.
No kernel may reach another device: no remote copies, remote signals or barrier semaphores. Data moves between devices by JAX's collectives and lax.ppermute only.
A program may use at most 64 MiB of HBM per device.

```python
import math
import jax
import jax.numpy as jnp
from jax import lax

D = 2048
HEAD = 128
SEQ = 64
EXAMPLES = 32
TOKENS = 2048


def block_levels(key, extent, shards, low, high):
    def one(axis_at, blocks):
        steps = jax.random.uniform(jax.random.fold_in(jax.random.fold_in(key, 6), axis_at), (blocks,), jnp.float32, low / len(shards), high / len(shards))
        return jnp.repeat(jnp.exp(steps), extent[axis_at] // blocks).reshape((-1,) + (1,) * (len(extent) - axis_at - 1))

    factor_of = one(*shards[0])
    for cut in shards[1:]:
        factor_of = factor_of * one(*cut)
    return factor_of


def scatter_about(stream_key, shape, width, bound, cuts=(), held_as=jnp.bfloat16):
    drawn = width * jax.random.normal(stream_key, shape, jnp.float32)
    if cuts:
        drawn = drawn * block_levels(stream_key, shape, cuts, -0.22, 0.18)
    return jnp.clip(drawn, -bound, bound).astype(held_as)


def setup_inputs(seed: int = 0, part: int = 0) -> dict:
    seeds = jax.random.split(jax.random.key(seed), 4)
    part_keys = jax.random.split(jax.random.fold_in(seeds[3], part), 4)
    layer_input = scatter_about(part_keys[0], (TOKENS, D), 1.0, 6.0, ((0, 16),))
    cotangent = scatter_about(part_keys[1], (TOKENS, 2 * HEAD), 1.0, 6.0, ((0, 16),))
    example_weight = jnp.clip(jnp.exp(math.log(4.0) - 2.306499 * jax.random.uniform(seeds[2], (EXAMPLES,), jnp.float32) ** block_levels(seeds[2], (EXAMPLES,), ((0, 16),), -0.2, 0.2)), 0.3984375, 4.0).astype(jnp.bfloat16)
    return dict(layer_input=layer_input, cotangent=cotangent, example_weight=example_weight)


def reference(layer_input, cotangent, example_weight):
    inputs = layer_input.astype(jnp.float32).reshape(EXAMPLES, SEQ, D)
    signals = cotangent.astype(jnp.float32).reshape(EXAMPLES, SEQ, 2 * HEAD)
    weights = example_weight.astype(jnp.float32)
    grads = jnp.einsum('esd,esh->edh', inputs, signals, precision=lax.Precision.HIGHEST)
    grads = grads * weights[:, None, None]
    flat = grads.reshape(EXAMPLES, D * 2 * HEAD)
    gram = jnp.dot(flat, flat.T, precision=lax.Precision.HIGHEST, preferred_element_type=jnp.float32)
    window = 2.0 * D * HEAD
    kernel = jnp.tril(gram, -1) / (SEQ * jnp.sqrt(window))
    sq_norms = jnp.diagonal(gram) / (SEQ * window)
    return (kernel, sq_norms)
```

```python
import functools

import jax
import jax.numpy as jnp
from jax import lax
from jax.experimental import pallas as pl
from jax.experimental.pallas import tpu as pltpu
from jax.sharding import PartitionSpec as P

LANES = 128


def swapped(value, distance):
    count = lax.axis_size("ex")
    return lax.ppermute(value, "ex", [(i, i ^ distance) for i in range(count)])


def dot_t(a, b):
    return lax.dot_general(a, b, (((1,), (1,)), ((), ())), preferred_element_type=jnp.float32)


def split_dot(a, b):
    high = a.astype(jnp.bfloat16)
    rest = a - high.astype(jnp.float32)
    middle = rest.astype(jnp.bfloat16)
    low = (rest - middle.astype(jnp.float32)).astype(jnp.bfloat16)
    parts = [jnp.dot(p, b, preferred_element_type=jnp.float32) for p in (high, middle, low)]
    return parts[0] + (parts[1] + parts[2])


def gram_kernel(devices, local_count, me_ref, weight_ref, *refs):
    chips, planes = devices // 2, devices // 4
    x_refs, refs = refs[:chips], refs[chips:]
    z_refs, refs = refs[:planes], refs[planes:]
    y_ref, core_ref, out_ref, x_all, c_all, rows_ref = refs
    chip_rows = x_refs[0].shape[0]
    tokens = chip_rows // 2
    examples = 2 * local_count
    seq_length = tokens // local_count

    for s in range(chips):
        x_all[s] = x_refs[s][...]
    for z in range(planes):
        c_all[2 * z, :tokens] = z_refs[z][...]
        c_all[2 * z + 1, :tokens] = y_ref[z]
        c_all[2 * z, tokens:] = core_ref[0, z]
        c_all[2 * z + 1, tokens:] = core_ref[1, z]
    rows_ref[...] = jnp.zeros_like(rows_ref)

    def block(i, j):
        product = dot_t(x_all[i], x_all[j]) * dot_t(c_all[i], c_all[j])
        summed = jnp.sum(product.reshape(examples, seq_length, chip_rows), axis=1)
        rows_ref[i, j, :examples] = summed

    if chips <= 8:
        for i in range(chips):
            for j in range(i + 1):
                block(i, j)
    else:

        @pl.loop(0, chips)
        def _(i):
            @pl.loop(0, i + 1)
            def _(j):
                block(i, j)

    held = rows_ref.shape[2]
    count = chips * examples
    row = lax.broadcasted_iota(jnp.int32, (chip_rows, LANES), 0)
    column = lax.broadcasted_iota(jnp.int32, (chip_rows, LANES), 1)
    lower = jnp.zeros((chips * held, LANES), jnp.float32)
    for j in range(chips):
        group = (row // seq_length + j * examples == column).astype(jnp.bfloat16)
        lower += split_dot(rows_ref[:, j].reshape(chips * held, chip_rows), group)
    lower = lower.reshape(chips, held, LANES)[:, :examples].reshape(count, LANES)
    square = lower if count == LANES else jnp.concatenate([lower, jnp.zeros((LANES - count, LANES), jnp.float32)])
    row = lax.broadcasted_iota(jnp.int32, (LANES, LANES), 0)
    column = lax.broadcasted_iota(jnp.int32, (LANES, LANES), 1)
    gram = square + jnp.where(row // examples < column // examples, square.T, 0.0)
    to_global = (jnp.bitwise_xor(row, me_ref[0] * local_count) == column).astype(jnp.bfloat16)
    gram = split_dot(gram[:count], to_global)
    out_ref[:, :8] = gram.reshape(planes, 8, LANES)
    out_ref[:, 8:] = jnp.broadcast_to(weight_ref[...], (planes, 8, LANES))


def body(layer_input, cotangent, example_weight):
    devices = lax.axis_size("ex")
    me = lax.axis_index("ex")
    chips, planes = devices // 2, devices // 4
    chip, core = me // 2, me % 2
    local_count = example_weight.shape[0]
    tokens, width = layer_input.shape
    seq_length = tokens // local_count
    window = width * cotangent.shape[1]
    own_width = width // devices
    weight = example_weight.astype(jnp.float32)

    cot = {0: cotangent}
    for z in range(planes - 1, 0, -1):
        cot[z] = swapped(cotangent, 4 * z)

    columns = layer_input.reshape(tokens, chips, 2, own_width)
    columns = jnp.transpose(columns, (2, 1, 0, 3))
    keep = lax.dynamic_index_in_dim(columns, core, 0, keepdims=False)
    give = lax.dynamic_index_in_dim(columns, 1 - core, 0, keepdims=False)
    got = swapped(give, 1)
    pair = jnp.stack([keep, got], axis=1).reshape(chips, 2 * tokens, own_width)
    mine = {}
    for s in [0] + list(range(chips - 1, 0, -1)):
        part = lax.dynamic_index_in_dim(pair, chip ^ s, 0, keepdims=False)
        mine[s] = swapped(part, 2 * s) if s else part

    over_z = jnp.stack([cot[z] for z in range(planes)])
    over_y = swapped(over_z, 2)
    over_core = swapped(jnp.stack([over_z, over_y]), 1)

    lane = lax.broadcasted_iota(jnp.int32, (8, LANES), 1)
    slot = lane - me * local_count
    sublane = lax.broadcasted_iota(jnp.int32, (8, LANES), 0)
    weight_row = jnp.zeros((8, LANES), jnp.float32)
    for k in range(local_count):
        weight_row = jnp.where((slot == k) & (sublane == 0), weight[k], weight_row)

    smem = pl.BlockSpec(memory_space=pltpu.SMEM)
    vmem = pl.BlockSpec(memory_space=pltpu.VMEM)
    operands = [mine[s] for s in range(chips)] + [cot[z] for z in range(planes)] + [over_y, over_core]
    partial = pl.pallas_call(
        functools.partial(gram_kernel, devices, local_count),
        out_shape=jax.ShapeDtypeStruct((planes, 16, LANES), jnp.float32),
        in_specs=[smem, vmem] + [vmem] * len(operands),
        out_specs=vmem,
        scratch_shapes=[
            pltpu.VMEM((chips, 2 * tokens, own_width), layer_input.dtype),
            pltpu.VMEM((chips, 2 * tokens, cotangent.shape[1]), cotangent.dtype),
            pltpu.VMEM((chips, chips, 8, 2 * tokens), jnp.float32),
        ],
        compiler_params=pltpu.CompilerParams(vmem_limit_bytes=48 * 1024 * 1024),
        name="gram",
    )(me.astype(jnp.int32).reshape(1), weight_row, *operands)

    total = partial[0]
    for z in range(planes - 1, 0, -1):
        total = total + swapped(partial[z], 4 * z)
    rows = local_count
    sums = jnp.concatenate([total[:rows], total[8:9]])
    for q in (3, 2, 1):
        sums = sums + swapped(jnp.concatenate([total[q * rows : (q + 1) * rows], total[8:9]]), q)

    count = devices * local_count
    grams = sums[:rows, :count] * (weight[:, None] * sums[rows : rows + 1, :count])
    own = (me * local_count + lax.iota(jnp.int32, local_count))[:, None]
    column = lax.iota(jnp.int32, count)[None, :]
    kernel = jnp.where(column < own, grams, 0.0) / (seq_length * jnp.sqrt(jnp.float32(window)))
    sq_norms = jnp.sum(jnp.where(column == own, grams, 0.0), axis=1) / (seq_length * jnp.float32(window))
    return (kernel, sq_norms)


def solution(mesh):
    placed = (P(("grp", "ex"), None), P(("grp", "ex"), None), P("ex"))
    return jax.shard_map(
        body,
        mesh=mesh,
        in_specs=placed,
        out_specs=(P(("grp", "ex"), None), P(("grp", "ex"))),
        check_vma=False,
    )
```

```python
import functools

import jax
import jax.numpy as jnp
from jax import lax
from jax.experimental import pallas as pl
from jax.experimental.pallas import tpu as pltpu
from jax.sharding import PartitionSpec as P

LANES = 128


def swapped(value, distance):
    count = lax.axis_size("ex")
    return lax.ppermute(value, "ex", [(i, i ^ distance) for i in range(count)])


def dot_t(a, b):
    return lax.dot_general(a, b, (((1,), (1,)), ((), ())), preferred_element_type=jnp.float32)


def three_parts(value, axis):
    high = value.astype(jnp.bfloat16)
    rest = value - high.astype(jnp.float32)
    middle = rest.astype(jnp.bfloat16)
    low = (rest - middle.astype(jnp.float32)).astype(jnp.bfloat16)
    return jnp.concatenate([high, middle, low], axis=axis)


def global_example(slot, place, far, local_count):
    distance, within = slot // local_count, slot % local_count
    return (2 * jnp.bitwise_xor(place[0], distance) + jnp.bitwise_xor(place[1], far)) * local_count + within


def order_kernel(local_count, seq_length, place, weight, own_spread, far_spread, gather_ref, weight_ref):
    for far, ref in enumerate((own_spread, far_spread)):
        token = lax.broadcasted_iota(jnp.int32, ref.shape, 0)
        lane = lax.broadcasted_iota(jnp.int32, ref.shape, 1)
        ref[...] = (global_example(token // seq_length, place, far, local_count) == lane).astype(ref.dtype)
    own = 2 * local_count
    row = lax.broadcasted_iota(jnp.int32, gather_ref.shape, 0)
    slot = lax.broadcasted_iota(jnp.int32, gather_ref.shape, 1)
    example = global_example(slot // 8 * own + slot % 8, place, 0, local_count)
    gather_ref[...] = ((example == row) & (slot % 8 < own)).astype(gather_ref.dtype)
    lane = lax.broadcasted_iota(jnp.int32, weight_ref.shape, 1) - (2 * place[0] + place[1]) * local_count
    weights = jnp.zeros(weight_ref.shape, jnp.float32)
    for k in range(local_count):
        weights = jnp.where(lane == k, weight[k], weights)
    weight_ref[...] = weights


def pair_sums(seq_length, rows_x, rows_c, far_x, far_c, spread, gather, sums_ref):
    groups, held, columns = sums_ref.shape
    span = columns // groups
    own = span // seq_length
    sums_ref[...] = jnp.zeros_like(sums_ref)

    def block(i, j, scale=None):
        product = dot_t(rows_x[i], far_x[j]) * dot_t(rows_c[i], far_c[j])
        summed = jnp.sum(product.reshape(own, seq_length, span), axis=1)
        if scale is not None:
            summed = summed * scale
        if isinstance(j, int):
            sums_ref[i, :own, j * span : (j + 1) * span] = summed
        else:
            sums_ref[i, :own, pl.ds(pl.multiple_of(j * span, span), span)] = summed

    if groups <= 4:
        for i in range(groups):
            block(i, i, 0.5)
            for j in range(i + 1, groups):
                block(i, j)
    else:

        @pl.loop(0, groups)
        def _(i):
            block(i, i, 0.5)

            @pl.loop(i + 1, groups)
            def _(j):
                block(i, j)

    count = groups * held
    parts = jnp.dot(
        three_parts(sums_ref[...].reshape(count, columns), 0), spread[...], preferred_element_type=jnp.float32
    )
    by_lane = parts[:count] + (parts[count : 2 * count] + parts[2 * count :])
    parts = jnp.dot(gather[...], three_parts(by_lane, 1), preferred_element_type=jnp.float32)
    return parts[:, :LANES] + (parts[:, LANES : 2 * LANES] + parts[:, 2 * LANES :])


def own_kernel(seq_length, x_ref, c_ref, spread, gather, out_ref, sums_ref):
    out_ref[...] = pair_sums(seq_length, x_ref, c_ref, x_ref, c_ref, spread, gather, sums_ref)


def far_kernel(
    seq_length, local_count, x_ref, c_ref, far_x, far_c, spread, gather, weight_ref, own_ref, out_ref, sums_ref
):
    half = own_ref[...] + pair_sums(seq_length, x_ref, c_ref, far_x, far_c, spread, gather, sums_ref)
    gram = half + half.T
    devices = out_ref.shape[0]
    out_ref[...] = jnp.broadcast_to(weight_ref[...], out_ref.shape)
    out_ref[:, :local_count] = gram[: devices * local_count].reshape(devices, local_count, LANES)


def output_kernel(local_count, kernel_scale, norm_scale, place, sums_ref, kernel_ref, norms_ref):
    total = jnp.sum(sums_ref[...], axis=0)
    weights = total[local_count : local_count + 1]
    shape = (local_count, LANES)
    own = (2 * place[0] + place[1]) * local_count + lax.broadcasted_iota(jnp.int32, shape, 0)
    lane = lax.broadcasted_iota(jnp.int32, shape, 1)
    mine = jnp.sum(jnp.where(lane == own, weights, 0.0), axis=1, keepdims=True)
    grams = total[:local_count] * (mine * weights)
    kernel_ref[...] = (jnp.where(lane < own, grams, 0.0) / kernel_scale)[:, : kernel_ref.shape[1]]
    norms = jnp.where(lane == own, grams, 0.0) / norm_scale
    square = jnp.concatenate([norms, jnp.zeros((LANES - local_count, LANES), jnp.float32)]).T
    norms_ref[...] = jnp.sum(square, axis=0, keepdims=True)[:, :local_count]


def body(layer_input, cotangent, example_weight):
    devices = lax.axis_size("ex")
    me = lax.axis_index("ex")
    chips, planes = devices // 2, devices // 4
    chip, core = me // 2, me % 2
    local_count = example_weight.shape[0]
    tokens, width = layer_input.shape
    seq_length = tokens // local_count
    heads = cotangent.shape[1]
    window = width * heads
    chip_width = width // chips
    weight = example_weight.astype(jnp.float32)

    smem = pl.BlockSpec(memory_space=pltpu.SMEM)
    vmem = pl.BlockSpec(memory_space=pltpu.VMEM)
    params = pltpu.CompilerParams(vmem_limit_bytes=24 * 1024 * 1024)

    array = jax.ShapeDtypeStruct
    place = jnp.stack([chip, core]).astype(jnp.int32)
    shapes = [array((chips * tokens, LANES), jnp.bfloat16)] * 2
    shapes += [array((LANES, planes * 8), jnp.bfloat16), array((8, LANES), jnp.float32)]
    own_spread, far_spread, gather, weight_row = pl.pallas_call(
        functools.partial(order_kernel, local_count, seq_length),
        out_shape=shapes,
        in_specs=[smem] * 2,
        out_specs=[vmem] * len(shapes),
        compiler_params=params,
        name="order_kernel",
    )(place, weight)

    cot = {0: cotangent}
    for z in range(planes - 1, 0, -1):
        cot[z] = swapped(cotangent, 4 * z)
    def columns(distance):
        return lax.dynamic_slice_in_dim(layer_input, (chip ^ distance) * chip_width, chip_width, 1)

    over_y = swapped(jnp.stack([columns(2 * z + 1) for z in range(planes)]), 2)
    over_y, order = lax.optimization_barrier((over_y, (own_spread, far_spread, gather, weight_row)))
    own_spread, far_spread, gather, weight_row = order
    mine = {}
    for z in range(planes - 1, -1, -1):
        part = jnp.concatenate([columns(2 * z), over_y[z]])
        mine[z] = swapped(part, 4 * z) if z else part
    over_z = jnp.stack([cot[z] for z in range(planes)])
    over_zy = swapped(over_z, 2)
    own_c = jnp.stack([over_z, over_zy], axis=1).reshape(planes, 2 * tokens, heads)
    far_c = jnp.stack([swapped(over_z, 1), swapped(over_zy, 1)], axis=1).reshape(planes, 2 * tokens, heads)
    own_x = jnp.stack([mine[z] for z in range(planes)])
    far_x = swapped(own_x, 1)

    sums = [pltpu.VMEM((planes, 8, chips * tokens), jnp.float32)]
    own = pl.pallas_call(
        functools.partial(own_kernel, seq_length),
        out_shape=array((LANES, LANES), jnp.float32),
        in_specs=[vmem] * 4,
        out_specs=vmem,
        scratch_shapes=sums,
        compiler_params=params,
        name="own_kernel",
    )(own_x, own_c, own_spread, gather)
    partial = pl.pallas_call(
        functools.partial(far_kernel, seq_length, local_count),
        out_shape=array((devices, 8, LANES), jnp.float32),
        in_specs=[vmem] * 8,
        out_specs=vmem,
        scratch_shapes=sums,
        compiler_params=params,
        name="far_kernel",
    )(own_x, own_c, far_x, far_c, far_spread, gather, weight_row, own)

    received = lax.all_to_all(partial, "ex", split_axis=0, concat_axis=0, tiled=True)
    scales = (seq_length * window**0.5, float(seq_length * window))
    count = devices * local_count
    kernel, sq_norms = pl.pallas_call(
        functools.partial(output_kernel, local_count, *scales),
        out_shape=[array((local_count, count), jnp.float32), array((1, local_count), jnp.float32)],
        in_specs=[smem, vmem],
        out_specs=[vmem] * 2,
        compiler_params=params,
        name="output_kernel",
    )(place, received)
    return (kernel, sq_norms.reshape(local_count))


def solution(mesh):
    placed = (P(("grp", "ex"), None), P(("grp", "ex"), None), P("ex"))
    return jax.shard_map(
        body,
        mesh=mesh,
        in_specs=placed,
        out_specs=(P(("grp", "ex"), None), P(("grp", "ex"))),
        check_vma=False,
    )
```

```python
import functools

import jax
import jax.numpy as jnp
from jax import lax
from jax.experimental import pallas as pl
from jax.experimental.pallas import tpu as pltpu
from jax.sharding import PartitionSpec as P

LANES = 128


def swapped(value, distance):
    count = lax.axis_size("ex")
    return lax.ppermute(value, "ex", [(i, i ^ distance) for i in range(count)])


def dot_t(a, b):
    return lax.dot_general(a, b, (((1,), (1,)), ((), ())), preferred_element_type=jnp.float32)


def three_parts(value, axis):
    high = value.astype(jnp.bfloat16)
    rest = value - high.astype(jnp.float32)
    middle = rest.astype(jnp.bfloat16)
    low = (rest - middle.astype(jnp.float32)).astype(jnp.bfloat16)
    return jnp.concatenate([high, middle, low], axis=axis)


def global_example(slot, place, far, local_count):
    distance, within = slot // local_count, slot % local_count
    return (2 * jnp.bitwise_xor(place[0], distance) + jnp.bitwise_xor(place[1], far)) * local_count + within


def order_kernel(local_count, seq_length, place, weight, own_spread, far_spread, gather_ref, weight_ref):
    examples = own_spread.shape[0] // seq_length
    lane = lax.broadcasted_iota(jnp.int32, (seq_length, LANES), 1)
    for far, ref in enumerate((own_spread, far_spread)):
        for slot in range(examples):
            example = global_example(slot, place, far, local_count)
            ref[slot * seq_length : (slot + 1) * seq_length] = (lane == example).astype(ref.dtype)
    own = 2 * local_count
    row = lax.broadcasted_iota(jnp.int32, gather_ref.shape, 0)
    slot = lax.broadcasted_iota(jnp.int32, gather_ref.shape, 1)
    example = global_example(slot // 8 * own + slot % 8, place, 0, local_count)
    gather_ref[...] = ((example == row) & (slot % 8 < own)).astype(gather_ref.dtype)
    lane = lax.broadcasted_iota(jnp.int32, weight_ref.shape, 1) - (2 * place[0] + place[1]) * local_count
    weights = jnp.zeros(weight_ref.shape, jnp.float32)
    for k in range(local_count):
        weights = jnp.where(lane == k, weight[k], weights)
    weight_ref[...] = weights


def pair_sums(seq_length, rows_x, rows_c, far_x, far_c, spread, gather, sums_ref):
    groups, held, columns = sums_ref.shape
    span = columns // groups
    own = span // seq_length
    sums_ref[...] = jnp.zeros_like(sums_ref)

    def block(i, j, scale=None):
        product = dot_t(rows_x[i], far_x[j]) * dot_t(rows_c[i], far_c[j])
        summed = jnp.sum(product.reshape(own, seq_length, span), axis=1)
        if scale is not None:
            summed = summed * scale
        if isinstance(j, int):
            sums_ref[i, :own, j * span : (j + 1) * span] = summed
        else:
            sums_ref[i, :own, pl.ds(pl.multiple_of(j * span, span), span)] = summed

    if groups <= 4:
        for i in range(groups):
            block(i, i, 0.5)
            for j in range(i + 1, groups):
                block(i, j)
    else:

        @pl.loop(0, groups)
        def _(i):
            block(i, i, 0.5)

            @pl.loop(i + 1, groups)
            def _(j):
                block(i, j)

    count = groups * held
    parts = jnp.dot(
        three_parts(sums_ref[...].reshape(count, columns), 0), spread[...], preferred_element_type=jnp.float32
    )
    by_lane = parts[:count] + (parts[count : 2 * count] + parts[2 * count :])
    parts = jnp.dot(gather[...], three_parts(by_lane, 1), preferred_element_type=jnp.float32)
    return parts[:, :LANES] + (parts[:, LANES : 2 * LANES] + parts[:, 2 * LANES :])


def own_kernel(seq_length, x_ref, c_ref, spread, gather, out_ref, sums_ref):
    out_ref[...] = pair_sums(seq_length, x_ref, c_ref, x_ref, c_ref, spread, gather, sums_ref)


def far_kernel(
    seq_length, local_count, x_ref, c_ref, far_x, far_c, spread, gather, weight_ref, own_ref, out_ref, sums_ref
):
    half = own_ref[...] + pair_sums(seq_length, x_ref, c_ref, far_x, far_c, spread, gather, sums_ref)
    gram = half + half.T
    devices = out_ref.shape[0]
    out_ref[...] = jnp.broadcast_to(weight_ref[: out_ref.shape[1]], out_ref.shape)
    out_ref[:, :local_count] = gram[: devices * local_count].reshape(devices, local_count, LANES)


def output_kernel(local_count, kernel_scale, norm_scale, place, sums_ref, kernel_ref, norms_ref):
    total = jnp.sum(sums_ref[...], axis=0)
    weights = total[local_count : local_count + 1]
    shape = (local_count, LANES)
    first = (2 * place[0] + place[1]) * local_count
    own = first + lax.broadcasted_iota(jnp.int32, shape, 0)
    lane = lax.broadcasted_iota(jnp.int32, shape, 1)
    mine = jnp.sum(jnp.where(lane == own, weights, 0.0), axis=1, keepdims=True)
    grams = total[:local_count] * (mine * weights)
    kernel_ref[...] = (jnp.where(lane < own, grams, 0.0) / kernel_scale)[:, : kernel_ref.shape[1]]
    norms = jnp.sum(jnp.where(lane == own, grams, 0.0), axis=0, keepdims=True) / norm_scale
    norms = jnp.broadcast_to(norms, (8, LANES))
    norms_ref[...] = pltpu.roll(norms, LANES - first, 1)[:1, :local_count]


def body(layer_input, cotangent, example_weight):
    devices = lax.axis_size("ex")
    me = lax.axis_index("ex")
    chips, planes = devices // 2, devices // 4
    chip, core = me // 2, me % 2
    local_count = example_weight.shape[0]
    tokens, width = layer_input.shape
    seq_length = tokens // local_count
    heads = cotangent.shape[1]
    window = width * heads
    chip_width = width // chips
    weight = example_weight.astype(jnp.float32)

    smem = pl.BlockSpec(memory_space=pltpu.SMEM)
    vmem = pl.BlockSpec(memory_space=pltpu.VMEM)
    params = pltpu.CompilerParams(vmem_limit_bytes=24 * 1024 * 1024)

    array = jax.ShapeDtypeStruct
    place = jnp.stack([chip, core]).astype(jnp.int32)
    shapes = [array((chips * tokens, LANES), jnp.bfloat16)] * 2
    shapes += [array((LANES, planes * 8), jnp.bfloat16), array((8, LANES), jnp.float32)]
    own_spread, far_spread, gather, weight_row = pl.pallas_call(
        functools.partial(order_kernel, local_count, seq_length),
        out_shape=shapes,
        in_specs=[smem] * 2,
        out_specs=[vmem] * len(shapes),
        compiler_params=params,
        name="order_kernel",
    )(place, weight)

    cot = {0: cotangent}
    for z in range(planes - 1, 0, -1):
        cot[z] = swapped(cotangent, 4 * z)
    def columns(distance):
        return lax.dynamic_slice_in_dim(layer_input, (chip ^ distance) * chip_width, chip_width, 1)

    moved = swapped(jnp.stack([columns(2 * z + 1) for z in range(1, planes)]), 2)
    moved, order = lax.optimization_barrier((moved, (own_spread, far_spread, gather, weight_row)))
    own_spread, far_spread, gather, weight_row = order
    over_y = {z: moved[z - 1] for z in range(1, planes)}
    over_y[0] = swapped(columns(1), 2)
    mine = {}
    for z in [z for z in range(2, planes)] + [1, 0]:
        part = jnp.concatenate([columns(2 * z), over_y[z]])
        if z == 1 and planes > 2:
            part, cot[planes - 1] = lax.optimization_barrier((part, cot[planes - 1]))
        mine[z] = swapped(part, 4 * z) if z else part
    over_z = jnp.stack([cot[z] for z in range(planes)])
    over_zy = swapped(over_z, 2)
    own_c = jnp.stack([over_z, over_zy], axis=1).reshape(planes, 2 * tokens, heads)
    far_c = jnp.stack([swapped(over_z, 1), swapped(over_zy, 1)], axis=1).reshape(planes, 2 * tokens, heads)
    own_x = jnp.stack([mine[z] for z in range(planes)])
    far_x = swapped(own_x, 1)

    sums = [pltpu.VMEM((planes, 8, chips * tokens), jnp.float32)]
    own = pl.pallas_call(
        functools.partial(own_kernel, seq_length),
        out_shape=array((LANES, LANES), jnp.float32),
        in_specs=[vmem] * 4,
        out_specs=vmem,
        scratch_shapes=sums,
        compiler_params=params,
        name="own_kernel",
    )(own_x, own_c, own_spread, gather)
    partial = pl.pallas_call(
        functools.partial(far_kernel, seq_length, local_count),
        out_shape=array((devices, 4, LANES), jnp.float32),
        in_specs=[vmem] * 8,
        out_specs=vmem,
        scratch_shapes=sums,
        compiler_params=params,
        name="far_kernel",
    )(own_x, own_c, far_x, far_c, far_spread, gather, weight_row, own)

    received = lax.all_to_all(partial, "ex", split_axis=0, concat_axis=0, tiled=True)
    scales = (seq_length * window**0.5, float(seq_length * window))
    count = devices * local_count
    kernel, sq_norms = pl.pallas_call(
        functools.partial(output_kernel, local_count, *scales),
        out_shape=[array((local_count, count), jnp.float32), array((1, local_count), jnp.float32)],
        in_specs=[smem, vmem],
        out_specs=[vmem] * 2,
        compiler_params=params,
        name="output_kernel",
    )(place, received)
    return (kernel, sq_norms.reshape(local_count))


def solution(mesh):
    placed = (P(("grp", "ex"), None), P(("grp", "ex"), None), P("ex"))
    return jax.shard_map(
        body,
        mesh=mesh,
        in_specs=placed,
        out_specs=(P(("grp", "ex"), None), P(("grp", "ex"))),
        check_vma=False,
    )
```

```python
import functools

import jax
import jax.numpy as jnp
from jax import lax
from jax.experimental import pallas as pl
from jax.experimental.pallas import tpu as pltpu
from jax.sharding import PartitionSpec as P

LANES = 128


def swapped(value, distance):
    count = lax.axis_size("ex")
    return lax.ppermute(value, "ex", [(i, i ^ distance) for i in range(count)])


def dot_t(a, b):
    return lax.dot_general(a, b, (((1,), (1,)), ((), ())), preferred_element_type=jnp.float32)


def three_parts(value, axis):
    high = value.astype(jnp.bfloat16)
    rest = value - high.astype(jnp.float32)
    middle = rest.astype(jnp.bfloat16)
    low = (rest - middle.astype(jnp.float32)).astype(jnp.bfloat16)
    return jnp.concatenate([high, middle, low], axis=axis)


def global_example(slot, place, far, local_count):
    distance, within = slot // local_count, slot % local_count
    return (2 * jnp.bitwise_xor(place[0], distance) + jnp.bitwise_xor(place[1], far)) * local_count + within


def order_kernel(
    local_count, seq_length, place, weight, own_spread, far_spread, gather_ref, weight_ref, below_ref, own_ref
):
    examples = own_spread.shape[0] // seq_length
    lane = lax.broadcasted_iota(jnp.int32, (seq_length, LANES), 1)
    for far, ref in enumerate((own_spread, far_spread)):
        for slot in range(examples):
            example = global_example(slot, place, far, local_count)
            ref[slot * seq_length : (slot + 1) * seq_length] = (lane == example).astype(ref.dtype)
    own = 2 * local_count
    row = lax.broadcasted_iota(jnp.int32, gather_ref.shape, 0)
    slot = lax.broadcasted_iota(jnp.int32, gather_ref.shape, 1)
    example = global_example(slot // 8 * own + slot % 8, place, 0, local_count)
    gather_ref[...] = ((example == row) & (slot % 8 < own)).astype(gather_ref.dtype)
    lane = lax.broadcasted_iota(jnp.int32, weight_ref.shape, 1) - (2 * place[0] + place[1]) * local_count
    weights = jnp.zeros(weight_ref.shape, jnp.float32)
    for k in range(local_count):
        weights = jnp.where(lane == k, weight[k], weights)
    weight_ref[...] = weights
    own = (2 * place[0] + place[1]) * local_count + lax.broadcasted_iota(jnp.int32, below_ref.shape, 0)
    lane = lax.broadcasted_iota(jnp.int32, below_ref.shape, 1)
    below_ref[...] = (lane < own).astype(jnp.float32)
    own_ref[...] = (lane == own).astype(jnp.float32)


def pair_sums(seq_length, rows_x, rows_c, far_x, far_c, spread, gather, sums_ref):
    groups, held, columns = sums_ref.shape
    span = columns // groups
    own = span // seq_length
    sums_ref[...] = jnp.zeros_like(sums_ref)

    def block(i, j, scale=None):
        product = dot_t(rows_x[i], far_x[j]) * dot_t(rows_c[i], far_c[j])
        summed = jnp.sum(product.reshape(own, seq_length, span), axis=1)
        if scale is not None:
            summed = summed * scale
        if isinstance(j, int):
            sums_ref[i, :own, j * span : (j + 1) * span] = summed
        else:
            sums_ref[i, :own, pl.ds(pl.multiple_of(j * span, span), span)] = summed

    if groups <= 4:
        for i in range(groups):
            block(i, i, 0.5)
            for j in range(i + 1, groups):
                block(i, j)
    else:

        @pl.loop(0, groups)
        def _(i):
            block(i, i, 0.5)

            @pl.loop(i + 1, groups)
            def _(j):
                block(i, j)

    count = groups * held
    parts = jnp.dot(
        three_parts(sums_ref[...].reshape(count, columns), 0), spread[...], preferred_element_type=jnp.float32
    )
    by_lane = parts[:count] + (parts[count : 2 * count] + parts[2 * count :])
    parts = jnp.dot(gather[...], three_parts(by_lane, 1), preferred_element_type=jnp.float32)
    return parts[:, :LANES] + (parts[:, LANES : 2 * LANES] + parts[:, 2 * LANES :])


def own_kernel(seq_length, x_ref, c_ref, spread, gather, out_ref, sums_ref):
    out_ref[...] = pair_sums(seq_length, x_ref, c_ref, x_ref, c_ref, spread, gather, sums_ref)


def far_kernel(
    seq_length, local_count, x_ref, c_ref, far_x, far_c, spread, gather, weight_ref, own_ref, out_ref, sums_ref
):
    half = own_ref[...] + pair_sums(seq_length, x_ref, c_ref, far_x, far_c, spread, gather, sums_ref)
    gram = half + half.T
    devices = out_ref.shape[0]
    out_ref[...] = jnp.broadcast_to(weight_ref[: out_ref.shape[1]], out_ref.shape)
    out_ref[:, :local_count] = gram[: devices * local_count].reshape(devices, local_count, LANES)


def output_kernel(local_count, kernel_scale, norm_scale, below, diagonal, sums_ref, kernel_ref, norms_ref):
    total = jnp.sum(sums_ref[...], axis=0)
    weights = total[local_count : local_count + 1]
    own = diagonal[:local_count]
    mine = jnp.sum(own * weights, axis=1, keepdims=True)
    grams = total[:local_count] * (mine * weights)
    kernel_ref[...] = ((grams * below[:local_count]) / kernel_scale)[:, : kernel_ref.shape[1]]
    norms = jnp.sum(grams * own, axis=1, keepdims=True) / norm_scale
    shape = (local_count, LANES)
    row, lane = (lax.broadcasted_iota(jnp.int32, shape, axis) for axis in (0, 1))
    norms_ref[...] = jnp.sum(jnp.where(row == lane, norms, 0.0), axis=0, keepdims=True)[:, :local_count]


def body(layer_input, cotangent, example_weight):
    devices = lax.axis_size("ex")
    me = lax.axis_index("ex")
    chips, planes = devices // 2, devices // 4
    chip, core = me // 2, me % 2
    local_count = example_weight.shape[0]
    tokens, width = layer_input.shape
    seq_length = tokens // local_count
    heads = cotangent.shape[1]
    window = width * heads
    chip_width = width // chips
    weight = example_weight.astype(jnp.float32)

    smem = pl.BlockSpec(memory_space=pltpu.SMEM)
    vmem = pl.BlockSpec(memory_space=pltpu.VMEM)
    params = pltpu.CompilerParams(vmem_limit_bytes=24 * 1024 * 1024)

    array = jax.ShapeDtypeStruct
    place = jnp.stack([chip, core]).astype(jnp.int32)
    cot = {0: cotangent}
    for z in range(planes - 1, 0, -1):
        cot[z] = swapped(cotangent, 4 * z)
    def columns(distance):
        return lax.dynamic_slice_in_dim(layer_input, (chip ^ distance) * chip_width, chip_width, 1)

    moved = swapped(jnp.stack([columns(2 * z + 1) for z in range(1, planes)]), 2)
    moved, place, weight = lax.optimization_barrier((moved, place, weight))
    over_y = {z: moved[z - 1] for z in range(1, planes)}
    shapes = [array((chips * tokens, LANES), jnp.bfloat16)] * 2
    shapes += [array((LANES, planes * 8), jnp.bfloat16)] + [array((8, LANES), jnp.float32)] * 3
    order = pl.pallas_call(
        functools.partial(order_kernel, local_count, seq_length),
        out_shape=shapes,
        in_specs=[smem] * 2,
        out_specs=[vmem] * len(shapes),
        compiler_params=params,
        name="order_kernel",
    )(place, weight)

    mine = {}
    for z in range(planes - 1, 0, -1):
        part = jnp.concatenate([columns(2 * z), over_y[z]])
        if z == 1 and planes > 2:
            part, cot[planes - 1] = lax.optimization_barrier((part, cot[planes - 1]))
        if z == 1:
            part, order = lax.optimization_barrier((part, order))
        mine[z] = swapped(part, 4 * z)
    over_z = jnp.stack([cot[z] for z in range(planes)])
    over_zy = swapped(over_z, 2)
    mine[0] = jnp.concatenate([columns(0), swapped(columns(1), 2)])
    other_z, other_zy = swapped(over_z, 1), swapped(over_zy, 1)
    own_c = jnp.stack([over_z, over_zy], axis=1).reshape(planes, 2 * tokens, heads)
    far_c = jnp.stack([other_z, other_zy], axis=1).reshape(planes, 2 * tokens, heads)
    own_spread, far_spread, gather, weight_row, below, diagonal = order
    own_x = jnp.stack([mine[z] for z in range(planes)])
    far_x = jnp.concatenate([swapped(own_x[:1], 1), swapped(own_x[1:], 1)])

    sums = [pltpu.VMEM((planes, 8, chips * tokens), jnp.float32)]
    own = pl.pallas_call(
        functools.partial(own_kernel, seq_length),
        out_shape=array((LANES, LANES), jnp.float32),
        in_specs=[vmem] * 4,
        out_specs=vmem,
        scratch_shapes=sums,
        compiler_params=params,
        name="own_kernel",
    )(own_x, own_c, own_spread, gather)
    partial = pl.pallas_call(
        functools.partial(far_kernel, seq_length, local_count),
        out_shape=array((devices, 4, LANES), jnp.float32),
        in_specs=[vmem] * 8,
        out_specs=vmem,
        scratch_shapes=sums,
        compiler_params=params,
        name="far_kernel",
    )(own_x, own_c, far_x, far_c, far_spread, gather, weight_row, own)

    received = lax.all_to_all(partial, "ex", split_axis=0, concat_axis=0, tiled=True)
    scales = (seq_length * window**0.5, float(seq_length * window))
    count = devices * local_count
    kernel, sq_norms = pl.pallas_call(
        functools.partial(output_kernel, local_count, *scales),
        out_shape=[array((local_count, count), jnp.float32), array((1, local_count), jnp.float32)],
        in_specs=[vmem] * 3,
        out_specs=[vmem] * 2,
        compiler_params=params,
        name="output_kernel",
    )(below, diagonal, received)
    return (kernel, sq_norms.reshape(local_count))


def solution(mesh):
    placed = (P(("grp", "ex"), None), P(("grp", "ex"), None), P("ex"))
    return jax.shard_map(
        body,
        mesh=mesh,
        in_specs=placed,
        out_specs=(P(("grp", "ex"), None), P(("grp", "ex"))),
        check_vma=False,
    )
```

```python
import functools

import jax
import jax.numpy as jnp
from jax import lax
from jax.experimental import pallas as pl
from jax.experimental.pallas import tpu as pltpu
from jax.sharding import PartitionSpec as P

LANES = 128


def swapped(value, distance):
    count = lax.axis_size("ex")
    return lax.ppermute(value, "ex", [(i, i ^ distance) for i in range(count)])


def dot_t(a, b):
    return lax.dot_general(a, b, (((1,), (1,)), ((), ())), preferred_element_type=jnp.float32)


def three_parts(value, axis):
    high = value.astype(jnp.bfloat16)
    rest = value - high.astype(jnp.float32)
    middle = rest.astype(jnp.bfloat16)
    low = (rest - middle.astype(jnp.float32)).astype(jnp.bfloat16)
    return jnp.concatenate([high, middle, low], axis=axis)


def global_example(slot, place, far, local_count):
    distance, within = slot // local_count, slot % local_count
    return (2 * jnp.bitwise_xor(place[0], distance) + jnp.bitwise_xor(place[1], far)) * local_count + within


def order_kernel(
    local_count, seq_length, place, weight, own_spread, far_spread, gather_ref, weight_ref, below_ref, own_ref
):
    examples = own_spread.shape[0] // seq_length
    lane = lax.broadcasted_iota(jnp.int32, (seq_length, LANES), 1)
    for far, ref in enumerate((own_spread, far_spread)):
        for slot in range(examples):
            example = global_example(slot, place, far, local_count)
            ref[slot * seq_length : (slot + 1) * seq_length] = (lane == example).astype(ref.dtype)
    own = 2 * local_count
    row = lax.broadcasted_iota(jnp.int32, gather_ref.shape, 0)
    slot = lax.broadcasted_iota(jnp.int32, gather_ref.shape, 1)
    example = global_example(slot // 8 * own + slot % 8, place, 0, local_count)
    gather_ref[...] = ((example == row) & (slot % 8 < own)).astype(gather_ref.dtype)
    lane = lax.broadcasted_iota(jnp.int32, weight_ref.shape, 1) - (2 * place[0] + place[1]) * local_count
    weights = jnp.zeros(weight_ref.shape, jnp.float32)
    for k in range(local_count):
        weights = jnp.where(lane == k, weight[:, k : k + 1].astype(jnp.float32), weights)
    weight_ref[...] = weights
    own = (2 * place[0] + place[1]) * local_count + lax.broadcasted_iota(jnp.int32, below_ref.shape, 0)
    lane = lax.broadcasted_iota(jnp.int32, below_ref.shape, 1)
    below_ref[...] = (lane < own).astype(jnp.float32)
    own_ref[...] = (lane == own).astype(jnp.float32)


def pair_sums(seq_length, rows_x, rows_c, far_x, far_c, spread, gather, sums_ref):
    groups, held, columns = sums_ref.shape
    span = columns // groups
    own = span // seq_length
    sums_ref[...] = jnp.zeros_like(sums_ref)

    def block(i, j, scale=None):
        product = dot_t(rows_x[i], far_x[j]) * dot_t(rows_c[i], far_c[j])
        summed = jnp.sum(product.reshape(own, seq_length, span), axis=1)
        if scale is not None:
            summed = summed * scale
        if isinstance(j, int):
            sums_ref[i, :own, j * span : (j + 1) * span] = summed
        else:
            sums_ref[i, :own, pl.ds(pl.multiple_of(j * span, span), span)] = summed

    if groups <= 4:
        for i in range(groups):
            block(i, i, 0.5)
            for j in range(i + 1, groups):
                block(i, j)
    else:

        @pl.loop(0, groups)
        def _(i):
            block(i, i, 0.5)

            @pl.loop(i + 1, groups)
            def _(j):
                block(i, j)

    count = groups * held
    parts = jnp.dot(
        three_parts(sums_ref[...].reshape(count, columns), 0), spread[...], preferred_element_type=jnp.float32
    )
    by_lane = parts[:count] + (parts[count : 2 * count] + parts[2 * count :])
    parts = jnp.dot(gather[...], three_parts(by_lane, 1), preferred_element_type=jnp.float32)
    return parts[:, :LANES] + (parts[:, LANES : 2 * LANES] + parts[:, 2 * LANES :])


def own_kernel(seq_length, x_ref, c_ref, spread, gather, out_ref, sums_ref):
    out_ref[...] = pair_sums(seq_length, x_ref, c_ref, x_ref, c_ref, spread, gather, sums_ref)


def far_kernel(
    seq_length, local_count, x_ref, c_ref, far_x, far_c, spread, gather, weight_ref, own_ref, out_ref, sums_ref
):
    half = own_ref[...] + pair_sums(seq_length, x_ref, c_ref, far_x, far_c, spread, gather, sums_ref)
    gram = half + half.T
    devices = out_ref.shape[0]
    out_ref[...] = jnp.broadcast_to(weight_ref[: out_ref.shape[1]], out_ref.shape)
    out_ref[:, :local_count] = gram[: devices * local_count].reshape(devices, local_count, LANES)


def output_kernel(local_count, kernel_scale, norm_scale, below, diagonal, sums_ref, kernel_ref, norms_ref):
    total = jnp.sum(sums_ref[...], axis=0)
    weights = total[local_count : local_count + 1]
    own = diagonal[:local_count]
    mine = jnp.sum(own * weights, axis=1, keepdims=True)
    grams = total[:local_count] * (mine * weights)
    kernel_ref[...] = ((grams * below[:local_count]) / kernel_scale)[:, : kernel_ref.shape[1]]
    norms = jnp.sum(grams * own, axis=1, keepdims=True) / norm_scale
    shape = (local_count, LANES)
    row, lane = (lax.broadcasted_iota(jnp.int32, shape, axis) for axis in (0, 1))
    norms_ref[...] = jnp.sum(jnp.where(row == lane, norms, 0.0), axis=0, keepdims=True)[:, :local_count]


def body(layer_input, cotangent, example_weight):
    devices = lax.axis_size("ex")
    me = lax.axis_index("ex")
    chips, planes = devices // 2, devices // 4
    chip, core = me // 2, me % 2
    local_count = example_weight.shape[0]
    tokens, width = layer_input.shape
    seq_length = tokens // local_count
    heads = cotangent.shape[1]
    window = width * heads
    chip_width = width // chips

    smem = pl.BlockSpec(memory_space=pltpu.SMEM)
    vmem = pl.BlockSpec(memory_space=pltpu.VMEM)
    params = pltpu.CompilerParams(vmem_limit_bytes=24 * 1024 * 1024)

    array = jax.ShapeDtypeStruct
    place = jnp.stack([chip, core]).astype(jnp.int32)
    cot = {0: cotangent}
    for z in range(planes - 1, 0, -1):
        cot[z] = swapped(cotangent, 4 * z)
    def columns(distance):
        return lax.dynamic_slice_in_dim(layer_input, (chip ^ distance) * chip_width, chip_width, 1)

    moved = swapped(jnp.stack([columns(2 * z + 1) for z in range(1, planes)]), 2)
    moved, place = lax.optimization_barrier((moved, place))
    over_y = {z: moved[z - 1] for z in range(1, planes)}
    shapes = [array((chips * tokens, LANES), jnp.bfloat16)] * 2
    shapes += [array((LANES, planes * 8), jnp.bfloat16)] + [array((8, LANES), jnp.float32)] * 3
    order = pl.pallas_call(
        functools.partial(order_kernel, local_count, seq_length),
        out_shape=shapes,
        in_specs=[smem, vmem],
        out_specs=[vmem] * len(shapes),
        compiler_params=params,
        name="order_kernel",
    )(place, example_weight.reshape(1, local_count))

    mine = {}
    for z in range(planes - 1, 0, -1):
        part = jnp.concatenate([columns(2 * z), over_y[z]])
        if z == 1 and planes > 2:
            part, cot[planes - 1] = lax.optimization_barrier((part, cot[planes - 1]))
        mine[z] = swapped(part, 4 * z)
    over_z = jnp.stack([cot[z] for z in range(planes)])
    over_zy = swapped(over_z, 2)
    other_z = swapped(over_z, 1)
    late, order = lax.optimization_barrier((columns(1), order))
    over_zy, other_z = lax.optimization_barrier((over_zy, other_z))
    mine[0] = jnp.concatenate([columns(0), swapped(late, 2)])
    other_zy = swapped(over_zy, 1)
    own_c = jnp.stack([over_z, over_zy], axis=1).reshape(planes, 2 * tokens, heads)
    far_c = jnp.stack([other_z, other_zy], axis=1).reshape(planes, 2 * tokens, heads)
    own_spread, far_spread, gather, weight_row, below, diagonal = order
    own_x = jnp.stack([mine[z] for z in range(planes)])
    far_x = swapped(own_x, 1)

    sums = [pltpu.VMEM((planes, 8, chips * tokens), jnp.float32)]
    own = pl.pallas_call(
        functools.partial(own_kernel, seq_length),
        out_shape=array((LANES, LANES), jnp.float32),
        in_specs=[vmem] * 4,
        out_specs=vmem,
        scratch_shapes=sums,
        compiler_params=params,
        name="own_kernel",
    )(own_x, own_c, own_spread, gather)
    partial = pl.pallas_call(
        functools.partial(far_kernel, seq_length, local_count),
        out_shape=array((devices, 4, LANES), jnp.float32),
        in_specs=[vmem] * 8,
        out_specs=vmem,
        scratch_shapes=sums,
        compiler_params=params,
        name="far_kernel",
    )(own_x, own_c, far_x, far_c, far_spread, gather, weight_row, own)

    received = lax.all_to_all(partial, "ex", split_axis=0, concat_axis=0, tiled=True)
    scales = (seq_length * window**0.5, float(seq_length * window))
    count = devices * local_count
    kernel, sq_norms = pl.pallas_call(
        functools.partial(output_kernel, local_count, *scales),
        out_shape=[array((local_count, count), jnp.float32), array((1, local_count), jnp.float32)],
        in_specs=[vmem] * 3,
        out_specs=[vmem] * 2,
        compiler_params=params,
        name="output_kernel",
    )(below, diagonal, received)
    return (kernel, sq_norms.reshape(local_count))


def solution(mesh):
    placed = (P(("grp", "ex"), None), P(("grp", "ex"), None), P("ex"))
    return jax.shard_map(
        body,
        mesh=mesh,
        in_specs=placed,
        out_specs=(P(("grp", "ex"), None), P(("grp", "ex"))),
        check_vma=False,
    )
```

```python
import functools

import jax
import jax.numpy as jnp
from jax import lax
from jax.experimental import pallas as pl
from jax.experimental.pallas import tpu as pltpu
from jax.sharding import PartitionSpec as P

LANES = 128


def swapped(value, distance):
    count = lax.axis_size("ex")
    return lax.ppermute(value, "ex", [(i, i ^ distance) for i in range(count)])


def dot_t(a, b):
    return lax.dot_general(a, b, (((1,), (1,)), ((), ())), preferred_element_type=jnp.float32)


def three_parts(value, axis):
    high = value.astype(jnp.bfloat16)
    rest = value - high.astype(jnp.float32)
    middle = rest.astype(jnp.bfloat16)
    low = (rest - middle.astype(jnp.float32)).astype(jnp.bfloat16)
    return jnp.concatenate([high, middle, low], axis=axis)


def global_example(slot, place, far, local_count):
    distance, within = slot // local_count, slot % local_count
    return (2 * jnp.bitwise_xor(place[0], distance) + jnp.bitwise_xor(place[1], far)) * local_count + within


def order_kernel(
    local_count, seq_length, place, weight, own_spread, far_spread, gather_ref, weight_ref, below_ref, own_ref
):
    examples = own_spread.shape[0] // seq_length
    lane = lax.broadcasted_iota(jnp.int32, (seq_length, LANES), 1)
    for far, ref in enumerate((own_spread, far_spread)):
        for slot in range(examples):
            example = global_example(slot, place, far, local_count)
            ref[slot * seq_length : (slot + 1) * seq_length] = (lane == example).astype(ref.dtype)
    own = 2 * local_count
    row = lax.broadcasted_iota(jnp.int32, gather_ref.shape, 0)
    slot = lax.broadcasted_iota(jnp.int32, gather_ref.shape, 1)
    example = global_example(slot // 8 * own + slot % 8, place, 0, local_count)
    gather_ref[...] = ((example == row) & (slot % 8 < own)).astype(gather_ref.dtype)
    lane = lax.broadcasted_iota(jnp.int32, weight_ref.shape, 1) - (2 * place[0] + place[1]) * local_count
    weights = jnp.zeros(weight_ref.shape, jnp.float32)
    for k in range(local_count):
        weights = jnp.where(lane == k, weight[k], weights)
    weight_ref[...] = weights
    own = (2 * place[0] + place[1]) * local_count + lax.broadcasted_iota(jnp.int32, below_ref.shape, 0)
    lane = lax.broadcasted_iota(jnp.int32, below_ref.shape, 1)
    below_ref[...] = (lane < own).astype(jnp.float32)
    own_ref[...] = (lane == own).astype(jnp.float32)


def pair_sums(seq_length, rows_x, rows_c, far_x, far_c, spread, gather, sums_ref):
    groups, held, columns = sums_ref.shape
    span = columns // groups
    own = span // seq_length
    sums_ref[...] = jnp.zeros_like(sums_ref)

    def block(i, j, scale=None):
        product = dot_t(rows_x[i], far_x[j]) * dot_t(rows_c[i], far_c[j])
        summed = jnp.sum(product.reshape(own, seq_length, span), axis=1)
        if scale is not None:
            summed = summed * scale
        if isinstance(j, int):
            sums_ref[i, :own, j * span : (j + 1) * span] = summed
        else:
            sums_ref[i, :own, pl.ds(pl.multiple_of(j * span, span), span)] = summed

    if groups <= 4:
        for i in range(groups):
            block(i, i, 0.5)
            for j in range(i + 1, groups):
                block(i, j)
    else:

        @pl.loop(0, groups)
        def _(i):
            block(i, i, 0.5)

            @pl.loop(i + 1, groups)
            def _(j):
                block(i, j)

    count = groups * held
    parts = jnp.dot(
        three_parts(sums_ref[...].reshape(count, columns), 0), spread[...], preferred_element_type=jnp.float32
    )
    by_lane = parts[:count] + (parts[count : 2 * count] + parts[2 * count :])
    parts = jnp.dot(gather[...], three_parts(by_lane, 1), preferred_element_type=jnp.float32)
    return parts[:, :LANES] + (parts[:, LANES : 2 * LANES] + parts[:, 2 * LANES :])


def own_kernel(seq_length, x_ref, c_ref, spread, gather, out_ref, sums_ref):
    out_ref[...] = pair_sums(seq_length, x_ref, c_ref, x_ref, c_ref, spread, gather, sums_ref)


def far_kernel(
    seq_length, local_count, x_ref, c_ref, far_x, far_c, spread, gather, weight_ref, own_ref, out_ref, sums_ref
):
    half = own_ref[...] + pair_sums(seq_length, x_ref, c_ref, far_x, far_c, spread, gather, sums_ref)
    gram = half + half.T
    devices = out_ref.shape[0]
    out_ref[...] = jnp.broadcast_to(weight_ref[: out_ref.shape[1]], out_ref.shape)
    out_ref[:, :local_count] = gram[: devices * local_count].reshape(devices, local_count, LANES)


def output_kernel(local_count, kernel_scale, norm_scale, below, diagonal, sums_ref, kernel_ref, norms_ref):
    total = jnp.sum(sums_ref[...], axis=0)
    weights = total[local_count : local_count + 1]
    own = diagonal[:local_count]
    mine = jnp.sum(own * weights, axis=1, keepdims=True)
    grams = total[:local_count] * (mine * weights)
    kernel_ref[...] = ((grams * below[:local_count]) / kernel_scale)[:, : kernel_ref.shape[1]]
    norms = jnp.sum(grams * own, axis=1, keepdims=True) / norm_scale
    shape = (local_count, LANES)
    row, lane = (lax.broadcasted_iota(jnp.int32, shape, axis) for axis in (0, 1))
    norms_ref[...] = jnp.sum(jnp.where(row == lane, norms, 0.0), axis=0, keepdims=True)[:, :local_count]


def body(layer_input, cotangent, example_weight):
    devices = lax.axis_size("ex")
    me = lax.axis_index("ex")
    chips, planes = devices // 2, devices // 4
    chip, core = me // 2, me % 2
    local_count = example_weight.shape[0]
    tokens, width = layer_input.shape
    seq_length = tokens // local_count
    heads = cotangent.shape[1]
    window = width * heads
    chip_width = width // chips
    weight = example_weight.astype(jnp.float32)

    smem = pl.BlockSpec(memory_space=pltpu.SMEM)
    vmem = pl.BlockSpec(memory_space=pltpu.VMEM)
    params = pltpu.CompilerParams(vmem_limit_bytes=24 * 1024 * 1024)

    array = jax.ShapeDtypeStruct
    place = jnp.stack([chip, core]).astype(jnp.int32)
    cot = {0: cotangent}
    for z in range(planes - 1, 0, -1):
        cot[z] = swapped(cotangent, 4 * z)
    def columns(distance):
        return lax.dynamic_slice_in_dim(layer_input, (chip ^ distance) * chip_width, chip_width, 1)

    moved = swapped(jnp.stack([columns(2 * z + 1) for z in range(1, planes)]), 2)
    moved, place, weight = lax.optimization_barrier((moved, place, weight))
    over_y = {z: moved[z - 1] for z in range(1, planes)}
    shapes = [array((chips * tokens, LANES), jnp.bfloat16)] * 2
    shapes += [array((LANES, planes * 8), jnp.bfloat16)] + [array((8, LANES), jnp.float32)] * 3
    order = pl.pallas_call(
        functools.partial(order_kernel, local_count, seq_length),
        out_shape=shapes,
        in_specs=[smem] * 2,
        out_specs=[vmem] * len(shapes),
        compiler_params=params,
        name="order_kernel",
    )(place, weight)

    mine = {}
    for z in range(planes - 1, 0, -1):
        part = jnp.concatenate([columns(2 * z), over_y[z]])
        if z == 1 and planes > 2:
            part, cot[planes - 1] = lax.optimization_barrier((part, cot[planes - 1]))
        mine[z] = swapped(part, 4 * z)
    over_z = jnp.stack([cot[z] for z in range(planes)])
    over_zy = swapped(over_z, 2)
    other_z = swapped(over_z, 1)
    late, order, cot[1] = lax.optimization_barrier((columns(1), order, cot[1]))
    over_zy, other_z = lax.optimization_barrier((over_zy, other_z))
    mine[0] = jnp.concatenate([columns(0), swapped(late, 2)])
    other_zy = swapped(over_zy, 1)
    own_c = jnp.stack([over_z, over_zy], axis=1).reshape(planes, 2 * tokens, heads)
    far_c = jnp.stack([other_z, other_zy], axis=1).reshape(planes, 2 * tokens, heads)
    own_spread, far_spread, gather, weight_row, below, diagonal = order
    own_x = jnp.stack([mine[z] for z in range(planes)])
    far_x = swapped(own_x, 1)

    sums = [pltpu.VMEM((planes, 8, chips * tokens), jnp.float32)]
    own = pl.pallas_call(
        functools.partial(own_kernel, seq_length),
        out_shape=array((LANES, LANES), jnp.float32),
        in_specs=[vmem] * 4,
        out_specs=vmem,
        scratch_shapes=sums,
        compiler_params=params,
        cost_estimate=pl.CostEstimate(flops=1, bytes_accessed=0, transcendentals=0),
        name="own_kernel",
    )(own_x, own_c, own_spread, gather)
    partial = pl.pallas_call(
        functools.partial(far_kernel, seq_length, local_count),
        out_shape=array((devices, 4, LANES), jnp.float32),
        in_specs=[vmem] * 8,
        out_specs=vmem,
        scratch_shapes=sums,
        compiler_params=params,
        cost_estimate=pl.CostEstimate(flops=1, bytes_accessed=0, transcendentals=0),
        name="far_kernel",
    )(own_x, own_c, far_x, far_c, far_spread, gather, weight_row, own)

    received = lax.all_to_all(partial, "ex", split_axis=0, concat_axis=0, tiled=True)
    scales = (seq_length * window**0.5, float(seq_length * window))
    count = devices * local_count
    kernel, sq_norms = pl.pallas_call(
        functools.partial(output_kernel, local_count, *scales),
        out_shape=[array((local_count, count), jnp.float32), array((1, local_count), jnp.float32)],
        in_specs=[vmem] * 3,
        out_specs=[vmem] * 2,
        compiler_params=params,
        name="output_kernel",
    )(below, diagonal, received)
    return (kernel, sq_norms.reshape(local_count))


def solution(mesh):
    placed = (P(("grp", "ex"), None), P(("grp", "ex"), None), P("ex"))
    return jax.shard_map(
        body,
        mesh=mesh,
        in_specs=placed,
        out_specs=(P(("grp", "ex"), None), P(("grp", "ex"))),
        check_vma=False,
    )
```

```python
import functools

import jax
import jax.numpy as jnp
from jax import lax
from jax.experimental import pallas as pl
from jax.experimental.pallas import tpu as pltpu
from jax.sharding import PartitionSpec as P

LANES = 128


def swapped(value, distance):
    count = lax.axis_size("ex")
    return lax.ppermute(value, "ex", [(i, i ^ distance) for i in range(count)])


def dot_t(a, b):
    return lax.dot_general(a, b, (((1,), (1,)), ((), ())), preferred_element_type=jnp.float32)


def three_parts(value, axis):
    high = value.astype(jnp.bfloat16)
    rest = value - high.astype(jnp.float32)
    middle = rest.astype(jnp.bfloat16)
    low = (rest - middle.astype(jnp.float32)).astype(jnp.bfloat16)
    return jnp.concatenate([high, middle, low], axis=axis)


def global_example(slot, place, far, local_count):
    distance, within = slot // local_count, slot % local_count
    return (2 * jnp.bitwise_xor(place[0], distance) + jnp.bitwise_xor(place[1], far)) * local_count + within


def order_kernel(
    local_count, seq_length, place, weight, own_spread, far_spread, gather_ref, weight_ref, below_ref, own_ref
):
    examples = own_spread.shape[0] // seq_length
    lane = lax.broadcasted_iota(jnp.int32, (seq_length, LANES), 1)
    for far, ref in enumerate((own_spread, far_spread)):
        for slot in range(examples):
            example = global_example(slot, place, far, local_count)
            ref[slot * seq_length : (slot + 1) * seq_length] = (lane == example).astype(ref.dtype)
    own = 2 * local_count
    row = lax.broadcasted_iota(jnp.int32, gather_ref.shape, 0)
    slot = lax.broadcasted_iota(jnp.int32, gather_ref.shape, 1)
    example = global_example(slot // 8 * own + slot % 8, place, 0, local_count)
    gather_ref[...] = ((example == row) & (slot % 8 < own)).astype(gather_ref.dtype)
    lane = lax.broadcasted_iota(jnp.int32, weight_ref.shape, 1) - (2 * place[0] + place[1]) * local_count
    weights = jnp.zeros(weight_ref.shape, jnp.float32)
    for k in range(local_count):
        weights = jnp.where(lane == k, weight[k], weights)
    weight_ref[...] = weights
    own = (2 * place[0] + place[1]) * local_count + lax.broadcasted_iota(jnp.int32, below_ref.shape, 0)
    lane = lax.broadcasted_iota(jnp.int32, below_ref.shape, 1)
    below_ref[...] = (lane < own).astype(jnp.float32)
    own_ref[...] = (lane == own).astype(jnp.float32)


def pair_sums(seq_length, rows_x, rows_c, far_x, far_c, spread, sums_ref):
    groups, held, columns = sums_ref.shape
    span = columns // groups
    own = span // seq_length
    sums_ref[...] = jnp.zeros_like(sums_ref)

    def block(i, j, scale=None):
        product = dot_t(rows_x[i], far_x[j]) * dot_t(rows_c[i], far_c[j])
        summed = jnp.sum(product.reshape(own, seq_length, span), axis=1)
        if scale is not None:
            summed = summed * scale
        if isinstance(j, int):
            sums_ref[i, :own, j * span : (j + 1) * span] = summed
        else:
            sums_ref[i, :own, pl.ds(pl.multiple_of(j * span, span), span)] = summed

    if groups <= 4:
        for i in range(groups):
            block(i, i, 0.5)
            for j in range(i + 1, groups):
                block(i, j)
    else:

        @pl.loop(0, groups)
        def _(i):
            block(i, i, 0.5)

            @pl.loop(i + 1, groups)
            def _(j):
                block(i, j)

    count = groups * held
    parts = jnp.dot(
        three_parts(sums_ref[...].reshape(count, columns), 0), spread[...], preferred_element_type=jnp.float32
    )
    return parts[:count] + (parts[count : 2 * count] + parts[2 * count :])


def own_kernel(seq_length, x_ref, c_ref, spread, out_ref, sums_ref):
    out_ref[...] = pair_sums(seq_length, x_ref, c_ref, x_ref, c_ref, spread, sums_ref)


def far_kernel(
    seq_length, local_count, x_ref, c_ref, far_x, far_c, spread, gather, weight_ref, own_ref, out_ref, sums_ref
):
    by_lane = own_ref[...] + pair_sums(seq_length, x_ref, c_ref, far_x, far_c, spread, sums_ref)
    parts = jnp.dot(gather[...], three_parts(by_lane, 1), preferred_element_type=jnp.float32)
    half = parts[:, :LANES] + (parts[:, LANES : 2 * LANES] + parts[:, 2 * LANES :])
    gram = half + half.T
    devices = out_ref.shape[0]
    out_ref[...] = jnp.broadcast_to(weight_ref[: out_ref.shape[1]], out_ref.shape)
    out_ref[:, :local_count] = gram[: devices * local_count].reshape(devices, local_count, LANES)


def output_kernel(local_count, kernel_scale, norm_scale, below, diagonal, sums_ref, kernel_ref, norms_ref):
    total = jnp.sum(sums_ref[...], axis=0)
    weights = total[local_count : local_count + 1]
    own = diagonal[:local_count]
    mine = jnp.sum(own * weights, axis=1, keepdims=True)
    grams = total[:local_count] * (mine * weights)
    kernel_ref[...] = ((grams * below[:local_count]) / kernel_scale)[:, : kernel_ref.shape[1]]
    norms = jnp.sum(grams * own, axis=1, keepdims=True) / norm_scale
    shape = (local_count, LANES)
    row, lane = (lax.broadcasted_iota(jnp.int32, shape, axis) for axis in (0, 1))
    norms_ref[...] = jnp.sum(jnp.where(row == lane, norms, 0.0), axis=0, keepdims=True)[:, :local_count]


def body(layer_input, cotangent, example_weight):
    devices = lax.axis_size("ex")
    me = lax.axis_index("ex")
    chips, planes = devices // 2, devices // 4
    chip, core = me // 2, me % 2
    local_count = example_weight.shape[0]
    tokens, width = layer_input.shape
    seq_length = tokens // local_count
    heads = cotangent.shape[1]
    window = width * heads
    chip_width = width // chips
    weight = example_weight.astype(jnp.float32)

    smem = pl.BlockSpec(memory_space=pltpu.SMEM)
    vmem = pl.BlockSpec(memory_space=pltpu.VMEM)
    params = pltpu.CompilerParams(vmem_limit_bytes=24 * 1024 * 1024)

    array = jax.ShapeDtypeStruct
    place = jnp.stack([chip, core]).astype(jnp.int32)
    cot = {0: cotangent}
    for z in range(planes - 1, 0, -1):
        cot[z] = swapped(cotangent, 4 * z)
    def columns(distance):
        return lax.dynamic_slice_in_dim(layer_input, (chip ^ distance) * chip_width, chip_width, 1)

    moved = swapped(jnp.stack([columns(2 * z + 1) for z in range(1, planes)]), 2)
    moved, place, weight = lax.optimization_barrier((moved, place, weight))
    over_y = {z: moved[z - 1] for z in range(1, planes)}
    shapes = [array((chips * tokens, LANES), jnp.bfloat16)] * 2
    shapes += [array((LANES, planes * 8), jnp.bfloat16)] + [array((8, LANES), jnp.float32)] * 3
    order = pl.pallas_call(
        functools.partial(order_kernel, local_count, seq_length),
        out_shape=shapes,
        in_specs=[smem] * 2,
        out_specs=[vmem] * len(shapes),
        compiler_params=params,
        name="order_kernel",
    )(place, weight)

    mine = {}
    for z in range(planes - 1, 0, -1):
        part = jnp.concatenate([columns(2 * z), over_y[z]])
        if z == 1 and planes > 2:
            part, cot[planes - 1] = lax.optimization_barrier((part, cot[planes - 1]))
        mine[z] = swapped(part, 4 * z)
    over_z = jnp.stack([cot[z] for z in range(planes)])
    over_zy = swapped(over_z, 2)
    other_z = swapped(over_z, 1)
    late, order, cot[1] = lax.optimization_barrier((columns(1), order, cot[1]))
    over_zy, other_z = lax.optimization_barrier((over_zy, other_z))
    mine[0] = jnp.concatenate([columns(0), swapped(late, 2)])
    other_zy = swapped(over_zy, 1)
    own_c = jnp.stack([over_z, over_zy], axis=1).reshape(planes, 2 * tokens, heads)
    far_c = jnp.stack([other_z, other_zy], axis=1).reshape(planes, 2 * tokens, heads)
    own_spread, far_spread, gather, weight_row, below, diagonal = order
    own_x = jnp.stack([mine[z] for z in range(planes)])
    far_x = swapped(own_x, 1)

    sums = [pltpu.VMEM((planes, 8, chips * tokens), jnp.float32)]
    own = pl.pallas_call(
        functools.partial(own_kernel, seq_length),
        out_shape=array((8 * planes, LANES), jnp.float32),
        in_specs=[vmem] * 3,
        out_specs=vmem,
        scratch_shapes=sums,
        compiler_params=params,
        cost_estimate=pl.CostEstimate(flops=1, bytes_accessed=0, transcendentals=0),
        name="own_kernel",
    )(own_x, own_c, own_spread)
    partial = pl.pallas_call(
        functools.partial(far_kernel, seq_length, local_count),
        out_shape=array((devices, 3, LANES), jnp.float32),
        in_specs=[vmem] * 8,
        out_specs=vmem,
        scratch_shapes=sums,
        compiler_params=params,
        cost_estimate=pl.CostEstimate(flops=1, bytes_accessed=0, transcendentals=0),
        name="far_kernel",
    )(own_x, own_c, far_x, far_c, far_spread, gather, weight_row, own)

    received = lax.all_to_all(partial, "ex", split_axis=0, concat_axis=0, tiled=True)
    scales = (seq_length * window**0.5, float(seq_length * window))
    count = devices * local_count
    kernel, sq_norms = pl.pallas_call(
        functools.partial(output_kernel, local_count, *scales),
        out_shape=[array((local_count, count), jnp.float32), array((1, local_count), jnp.float32)],
        in_specs=[vmem] * 3,
        out_specs=[vmem] * 2,
        compiler_params=params,
        name="output_kernel",
    )(below, diagonal, received)
    return (kernel, sq_norms.reshape(local_count))


def solution(mesh):
    placed = (P(("grp", "ex"), None), P(("grp", "ex"), None), P("ex"))
    return jax.shard_map(
        body,
        mesh=mesh,
        in_specs=placed,
        out_specs=(P(("grp", "ex"), None), P(("grp", "ex"))),
        check_vma=False,
    )
```
